32 devices in a mesh: row: 2 (over core), mesh: 16 (over z, y, x).
Axes of the slice: x: 2, y: 2, z: 4, core: 2. Of those that a mesh axis runs over, the one named last changes fastest.
Arguments:
- state: float32 [2, 7, 5, 512, 256], P('row', None, None, 'mesh'), may hold values from -6 to 6
- inverse_blocks: float32 [2, 5, 5, 512, 256], P('row', None, None, 'mesh'), may hold values from -0.25 to 0.5
- flux_jacobian: float32 [2, 5, 5], P('row'), may hold values from -2.5 to 2.5
- harmonics: int32 [2, 3], replicated, may hold values from 1 to 17, as said below
- interface_delay: float32 [2], replicated, may hold values from 0 to 1
- inflow: float32 [7, 5, 512], P(None, None, 'mesh'), may hold values from -6 to 6
- pairing: int32 [2, 512], P('row', 'mesh'), may hold values from 0 to 511, as said below
Outputs:
- updated: float32 [2, 7, 5, 512, 256], P('row', None, None, 'mesh')
The draws below stay inside these ranges and needn't reach their ends.
Inputs may be any that keep to these rules, and one draw needn't show every extreme that they name: `harmonics`: each row's harmonic numbers leave the remainders 1 to 3 in some order when divided by 7. `pairing`: within each aligned block of 32 lines, a permutation of that block's lines.
All inputs are finite; a program needn't handle non-finite values.
Results may differ from the reference program's by a relative error of at most 0.00016.
Values sent between devices are 32-bit elements; how exact they have to be, the bound alone decides.
A program may use at most 64 MiB of HBM per device.

```python
import jax
import jax.numpy as jnp
from jax import lax

HARMONICS = 3
TIME_SAMPLES = 7
VARIABLES = 5
SECTIONS = 3
LINE_CELLS = 256
LINES_DEV = 32
LINES = 512
BLADE_ROWS = 2


def draw_harmonics(key, part):
    split_keys = jax.random.split(key, 2)
    scores = jax.random.randint(split_keys[0], (BLADE_ROWS, HARMONICS), 0, 1 << 20) * HARMONICS + jnp.arange(HARMONICS, dtype=jnp.int32)[None, :]
    remainders = jnp.argsort(scores, axis=1).astype(jnp.int32) + 1
    multiples = jax.random.randint(split_keys[1], (BLADE_ROWS, HARMONICS), 0, 3).astype(jnp.int32)
    first_row = jnp.where(remainders[0] == HARMONICS, 2, jnp.where(remainders[0] == 1, 0, multiples[0])).astype(jnp.int32)
    multiples = multiples.at[0].set(first_row)
    return (remainders + TIME_SAMPLES * multiples).astype(jnp.int32)


def draw_pairing(key, part):
    block_count = LINES // LINES_DEV
    scores = jax.random.randint(key, (BLADE_ROWS, block_count, LINES_DEV), 0, 1 << 20) * LINES_DEV + jnp.arange(LINES_DEV, dtype=jnp.int32)[None, None, :]
    ordering = jnp.argsort(scores, axis=2).astype(jnp.int32)
    ordering = ordering + (jnp.arange(block_count, dtype=jnp.int32) * LINES_DEV)[None, :, None]
    return ordering.reshape(BLADE_ROWS, LINES).astype(jnp.int32)


def draw_inverse_blocks(key, part):
    split_keys = jax.random.split(key, 2)
    shape_diag = (BLADE_ROWS, VARIABLES, LINES, LINE_CELLS)
    shape_full = (BLADE_ROWS, VARIABLES, VARIABLES, LINES, LINE_CELLS)
    diagonal_part = jnp.exp(jax.random.uniform(split_keys[0], shape_diag, jnp.float32, jnp.log(0.15), jnp.log(0.45)))
    off_diagonal = jnp.clip(jax.random.normal(split_keys[1], shape_full, jnp.float32), -4.0, 4.0) * 0.06
    identity_mask = jnp.eye(VARIABLES, dtype=jnp.float32)[None, :, :, None, None]
    return (identity_mask * diagonal_part[:, :, None, :, :] + (1.0 - identity_mask) * off_diagonal).astype(jnp.float32)


def levels(key, dims, shards, smallest, top_value):
    loudness = 1.0
    for axis_at, shards_of in shards:
        steps = jax.random.uniform(jax.random.fold_in(jax.random.fold_in(key, 6), axis_at), (shards_of,), jnp.float32, smallest / len(shards), top_value / len(shards))
        loudness = loudness * jnp.repeat(jnp.exp(steps), dims[axis_at] // shards_of).reshape((-1,) + (1,) * (len(dims) - 1 - axis_at))
    return loudness


def bell_draw(rng, shape, spread, reach, cuts=(), kind=jnp.bfloat16):
    values = spread * jax.random.normal(rng, shape, jnp.float32)
    if cuts:
        values = values * levels(rng, shape, cuts, -0.22, 0.18)
    return jnp.clip(values, -reach, reach).astype(kind)


def setup_inputs(seed: int = 0) -> dict:
    keys = jax.random.split(jax.random.key(seed), 8)
    state = bell_draw(keys[0], (BLADE_ROWS, TIME_SAMPLES, VARIABLES, LINES, LINE_CELLS), 1.0, 6.0, ((0, 2), (3, 16)), jnp.float32)
    inverse_blocks = draw_inverse_blocks(jax.random.fold_in(keys[7], 71), 0)
    flux_jacobian = bell_draw(keys[2], (BLADE_ROWS, VARIABLES, VARIABLES), VARIABLES ** -0.5, 2.5, ((0, 2),), jnp.float32)
    harmonics = draw_harmonics(jax.random.fold_in(keys[7], 71), 0)
    interface_delay = jnp.clip(jax.random.uniform(keys[4], (BLADE_ROWS,), jnp.float32, 0.0, 1.0), 0.0, 1.0)
    inflow = bell_draw(keys[5], (TIME_SAMPLES, VARIABLES, LINES), 1.0, 6.0, ((2, 16),), jnp.float32)
    pairing = draw_pairing(jax.random.fold_in(keys[7], 71), 0)
    return {"state": state, "inverse_blocks": inverse_blocks, "flux_jacobian": flux_jacobian, "harmonics": harmonics, "interface_delay": interface_delay, "inflow": inflow, "pairing": pairing}


largest_mode = lax.Precision.HIGHEST
nu_second = 0.25
nu_fourth = 0.03
time_scale = 0.05


def spectral_basis(sample_times, harmonic_modes):
    phase_angles = 2.0 * jnp.pi * sample_times[:, None] * harmonic_modes[None, :].astype(jnp.float32)
    column_of_ones = jnp.ones((sample_times.shape[0], 1), jnp.float32)
    return jnp.concatenate([column_of_ones, jnp.cos(phase_angles), jnp.sin(phase_angles)], axis=1)


def basis_derivative(sample_times, harmonic_modes):
    angular_speeds = 2.0 * jnp.pi * harmonic_modes.astype(jnp.float32)
    phase_angles = sample_times[:, None] * angular_speeds[None, :]
    column_of_zeros = jnp.zeros((sample_times.shape[0], 1), jnp.float32)
    return jnp.concatenate([column_of_zeros, -angular_speeds[None, :] * jnp.sin(phase_angles), angular_speeds[None, :] * jnp.cos(phase_angles)], axis=1)


def forward_transform(sample_times, harmonic_modes):
    sample_count = sample_times.shape[0]
    mode_weights = jnp.concatenate([jnp.full((1,), 1.0 / sample_count, jnp.float32), jnp.full((sample_count - 1,), 2.0 / sample_count, jnp.float32)])
    return mode_weights[:, None] * spectral_basis(sample_times, harmonic_modes).T


def row_operators(harmonics, interface_delay, blade_row_index):
    sample_times = jnp.arange(TIME_SAMPLES, dtype=jnp.float32) / TIME_SAMPLES
    local_modes = harmonics[blade_row_index]
    upstream_modes = harmonics[jnp.maximum(blade_row_index - 1, 0)]
    spectral_derivative = jnp.dot(basis_derivative(sample_times, local_modes), forward_transform(sample_times, local_modes), precision=largest_mode, preferred_element_type=jnp.float32)
    interface_mapping = jnp.dot(spectral_basis(sample_times + interface_delay[blade_row_index], upstream_modes), forward_transform(sample_times, upstream_modes), precision=largest_mode, preferred_element_type=jnp.float32)
    return spectral_derivative, interface_mapping


def section_residual(padded, ghost_cells, spectral_derivative, flux_jac):
    centre = padded[:, :, 2:-2]
    before = jnp.concatenate([ghost_cells[:, :, :, None], centre[:, :, :, :-1]], axis=3)
    advection = jnp.einsum('ab,tbwl->tawl', flux_jac, centre - before, precision=largest_mode)
    second_diff = padded[:, :, 3:-1] - 2.0 * centre + padded[:, :, 1:-3]
    fourth_diff = padded[:, :, 4:] - 4.0 * padded[:, :, 3:-1] + 6.0 * centre - 4.0 * padded[:, :, 1:-3] + padded[:, :, :-4]
    temporal = jnp.einsum('ts,svwl->tvwl', spectral_derivative, centre, precision=largest_mode)
    return advection - nu_second * second_diff + nu_fourth * fourth_diff + time_scale * temporal


def apply_block(inverse, residual):
    total = inverse[None, :, 0] * residual[:, 0][:, None]
    for column_index in range(1, inverse.shape[1]):
        total = total + inverse[None, :, column_index] * residual[:, column_index][:, None]
    return total


def reference(state, inverse_blocks, flux_jacobian, harmonics, interface_delay, inflow, pairing):
    outlet = state[:, :, :, :, -1]
    results = []
    for blade_row_index in range(BLADE_ROWS):
        spectral_derivative, interface_mapping = row_operators(harmonics, interface_delay, blade_row_index)
        upstream = inflow if blade_row_index == 0 else outlet[blade_row_index - 1]
        paired = jnp.take(upstream, pairing[blade_row_index], axis=2)
        ghost_cells = jnp.einsum('ts,svw->tvw', interface_mapping, paired, precision=largest_mode)
        base_state = state[blade_row_index]
        current = base_state
        for section_index in range(SECTIONS):
            padded = jnp.pad(current, ((0, 0), (0, 0), (2, 2), (0, 0)))
            residual = section_residual(padded, ghost_cells, spectral_derivative, flux_jacobian[blade_row_index])
            section_weight = (section_index + 1.0) / SECTIONS
            current = base_state - section_weight * apply_block(inverse_blocks[blade_row_index], residual)
        results.append(current)
    return jnp.stack(results)
```

```python
import functools
import math

import jax
import jax.numpy as jnp
from jax import lax
from jax.experimental import pallas as pl
from jax.experimental.pallas import tpu as pltpu
from jax.sharding import PartitionSpec as P

SECTIONS = 3
nu_second = 0.25
nu_fourth = 0.03
time_scale = 0.05
LANES = 128
SUB = 8
PAD = 8
HALO = 2
MESH = pl.DeviceIdType.MESH


def derivative_coefficients(harm, row, samples, count):
    modes = [harm[row, j] for j in range(count)]
    result = []
    for d in range(1, samples // 2 + 1):
        total = jnp.float32(0.0)
        for n in modes:
            left = lax.rem(n, jnp.int32(samples))
            sine = jnp.float32(0.0)
            for r in range(1, count + 1):
                value = math.sin(2.0 * math.pi * ((r * d) % samples) / samples)
                sine = jnp.where(left == r, jnp.float32(value), sine)
            total = total + n.astype(jnp.float32) * sine
        result.append(total * jnp.float32(-4.0 * math.pi / samples))
    return result


def transfer_matrix(harm, upstream, delay, samples, variables, count):
    used = samples * variables
    high = -(-used // SUB) * SUB
    i = lax.broadcasted_iota(jnp.int32, (high, LANES), 0)
    j = lax.broadcasted_iota(jnp.int32, (high, LANES), 1)
    t = j // variables
    s = i // variables
    same = (i - s * variables == j - t * variables) & (i < used) & (j < used)
    total = jnp.full((high, LANES), 1.0 / samples, jnp.float32)
    for k in range(count):
        n = harm[upstream, k]
        shift = n.astype(jnp.float32) * delay
        steps = n * (t - s + samples)
        steps = steps - samples * (steps // samples)
        turns = steps.astype(jnp.float32) * (1.0 / samples) + shift
        turns = turns - jnp.floor(turns)
        total = total + (2.0 / samples) * jnp.cos((2.0 * math.pi) * turns)
    total = jnp.where(same, total, 0.0)
    return jnp.concatenate([total, jnp.zeros((LANES - high, LANES), jnp.float32)], axis=0)


def kernel(rows, n, samples, variables, count,
           state, inverse, flux, harm, delay, inflow, pairing, out,
           q0, qa, qb, iv, ghost, mixing, xout, xin, flow, send, recv,
           load_sem, iv_sem, out_sem, send_sem, recv_sem, xsend_sem, xrecv_sem):
    halves, _, _, lines, _ = iv.shape[0], iv.shape[1], iv.shape[2], iv.shape[3], iv.shape[4]
    tv = samples * variables
    tiles = lines // SUB
    row = lax.axis_index("row")
    me = lax.axis_index("mesh")
    has_down = me > 0
    has_up = me < n - 1
    has_before = row > 0
    has_after = row < rows - 1
    down, up, before, after = {"mesh": me - 1}, {"mesh": me + 1}, {"row": row - 1}, {"row": row + 1}
    ways = ((has_down, down), (has_up, up), (has_before, before), (has_after, after))

    barrier = pltpu.get_barrier_semaphore()
    for ok, where in ways:
        @pl.when(ok)
        def _(where=where):
            pl.semaphore_signal(barrier, inc=1, device_id=where, device_id_type=MESH)

    loads = [
        pltpu.make_async_copy(
            state.at[:, :, pl.ds(h * LANES, LANES)],
            q0.at[h, :, pl.ds(PAD, lines), :],
            load_sem.at[h],
        )
        for h in range(halves)
    ]
    iv_loads = [
        pltpu.make_async_copy(
            inverse.at[:, :, :, pl.ds(h * LANES, LANES)], iv.at[h], iv_sem.at[h]
        )
        for h in range(halves)
    ]
    for copy in reversed(loads):
        copy.start()
    for copy in iv_loads:
        copy.start()

    zeros = jnp.zeros((tv, PAD, LANES), jnp.float32)
    for q in (qa, qb, q0):
        for h in range(halves):
            q[h, :, 0:PAD, :] = zeros
            q[h, :, PAD + lines : 2 * PAD + lines, :] = zeros

    for copy in reversed(loads):
        copy.wait()

    lane = lax.broadcasted_iota(jnp.int32, (lines, LANES), 1)
    packed = jnp.zeros((lines, LANES), jnp.float32)
    for i in range(tv):
        column = pltpu.roll(q0[halves - 1, i, PAD : PAD + lines, :], (i + 1) % LANES, 1)
        packed = jnp.where(lane == i, column, packed)
    xout[...] = packed

    def copies(s):
        first = pltpu.make_async_remote_copy(
            src_ref=send.at[s, 0], dst_ref=recv.at[s, 1], send_sem=send_sem.at[s, 0],
            recv_sem=recv_sem.at[s, 1], device_id=down, device_id_type=MESH)
        last = pltpu.make_async_remote_copy(
            src_ref=send.at[s, 1], dst_ref=recv.at[s, 0], send_sem=send_sem.at[s, 1],
            recv_sem=recv_sem.at[s, 0], device_id=up, device_id_type=MESH)
        return first, last

    def pack(s, q):
        for h in range(halves):
            send[s, 0, h] = q[h, :, PAD : PAD + HALO, :]
            send[s, 1, h] = q[h, :, PAD + lines - HALO : PAD + lines, :]

    def start(s):
        first, last = copies(s)
        pl.when(has_down)(first.start)
        pl.when(has_up)(last.start)

    def finish(s, q):
        first, last = copies(s)

        @pl.when(has_down)
        def _():
            last.wait_recv()
            for h in range(halves):
                q[h, :, PAD - HALO : PAD, :] = recv[s, 0, h]

        @pl.when(has_up)
        def _():
            first.wait_recv()
            for h in range(halves):
                q[h, :, PAD + lines : PAD + lines + HALO, :] = recv[s, 1, h]

    pack(0, q0)
    across = pltpu.make_async_remote_copy(
        src_ref=xout, dst_ref=xin, send_sem=xsend_sem, recv_sem=xrecv_sem,
        device_id=after, device_id_type=MESH)

    greeted = sum(ok.astype(jnp.int32) for ok, _ in ways)
    pl.semaphore_wait(barrier, greeted)
    pl.when(has_after)(across.start)
    start(0)

    weights = [(s + 1.0) / SECTIONS for s in range(SECTIONS)]
    for s in range(SECTIONS):
        for b in range(variables):
            for a in range(variables):
                mixing[s, b, a] = jnp.full((SUB, LANES), flux[0, a, b] * jnp.float32(weights[s]), jnp.float32)
    slopes = derivative_coefficients(harm, row, samples, count)
    to_ghost = transfer_matrix(harm, jnp.maximum(row - 1, 0), delay[row], samples, variables, count)
    chosen = (
        jnp.broadcast_to(pairing[...] - me * lines, (lines, lines))
        == lax.broadcasted_iota(jnp.int32, (lines, lines), 0)
    ).astype(jnp.float32)

    @pl.when(row == 0)
    def _():
        flow[...] = jnp.zeros((LANES, LANES), jnp.float32)
        for t in range(samples):
            flow[t * variables : (t + 1) * variables, 0:lines] = inflow[t]
        xin[...] = jnp.transpose(flow[...])[0:lines, :]

    @pl.when(has_before)
    def _():
        across.wait_recv()

    paired = lax.dot_general(
        chosen, xin[...], (((0,), (0,)), ((), ())),
        precision=lax.Precision.HIGHEST, preferred_element_type=jnp.float32)
    shifted = jnp.dot(
        paired, to_ghost, precision=lax.Precision.HIGHEST, preferred_element_type=jnp.float32)
    for i in range(tv):
        ghost[i] = pltpu.roll(shifted, (LANES - i) % LANES, 1)
    for copy in iv_loads:
        copy.wait()

    at_start = lax.broadcasted_iota(jnp.int32, (variables, SUB, LANES), 2) == 0

    def tile(s, k, src, dst):
        w = weights[s]
        k0 = jnp.float32(w * (2.0 * nu_second + 6.0 * nu_fourth))
        k1 = jnp.float32(w * (-nu_second - 4.0 * nu_fourth))
        k2 = jnp.float32(w * nu_fourth)
        turn = [e * jnp.float32(time_scale * w) for e in slopes]
        base = pl.multiple_of(PAD + k * SUB, SUB)
        line = pl.multiple_of(k * SUB, SUB)
        for t in range(samples):
            own = pl.ds(t * variables, variables)
            lower = ghost[own, pl.ds(line, SUB), :]
            for h in range(halves):
                centre = src[h, own, pl.ds(base, SUB), :]
                rolled = pltpu.roll(centre, 1, 2)
                step = centre - jnp.where(at_start, lower, rolled)
                lower = rolled
                total = k0 * centre
                total = total + k1 * (src[h, own, pl.ds(base - 1, SUB), :] + src[h, own, pl.ds(base + 1, SUB), :])
                total = total + k2 * (src[h, own, pl.ds(base - 2, SUB), :] + src[h, own, pl.ds(base + 2, SUB), :])
                for d, slope in enumerate(turn, 1):
                    earlier = pl.ds(((t - d) % samples) * variables, variables)
                    later = pl.ds(((t + d) % samples) * variables, variables)
                    total = total + slope * (
                        src[h, earlier, pl.ds(base, SUB), :] - src[h, later, pl.ds(base, SUB), :])
                for b in range(variables):
                    total = total + mixing[s, b] * step[b : b + 1]
                new = q0[h, own, pl.ds(base, SUB), :]
                for c in range(variables):
                    new = new - iv[h, :, c, pl.ds(line, SUB), :] * total[c : c + 1]
                dst[h, own, pl.ds(base, SUB), :] = new

    def inner(s, src, dst):
        @pl.loop(1, tiles - 1)
        def _(k):
            tile(s, k, src, dst)

    def outer(s, src, dst):
        @pl.loop(0, 2)
        def _(i):
            tile(s, i * (tiles - 1), src, dst)

    inner(0, q0, qa)
    finish(0, q0)
    outer(0, q0, qa)
    pack(1, qa)
    start(1)
    inner(1, qa, qb)
    finish(1, qa)
    outer(1, qa, qb)
    pack(2, qb)
    start(2)
    inner(2, qb, qa)
    finish(2, qb)
    outer(2, qb, qa)

    stores = [
        pltpu.make_async_copy(
            qa.at[h, :, pl.ds(PAD, lines), :],
            out.at[:, :, pl.ds(h * LANES, LANES)],
            out_sem.at[h],
        )
        for h in range(halves)
    ]
    for copy in stores:
        copy.start()
    for s in range(SECTIONS):
        first, last = copies(s)
        pl.when(has_down)(first.wait_send)
        pl.when(has_up)(last.wait_send)
    pl.when(has_after)(across.wait_send)
    for copy in stores:
        copy.wait()


def body(rows, n, state, inverse_blocks, flux_jacobian, harmonics, interface_delay, inflow, pairing):
    _, samples, variables, lines, cells = state.shape
    count = harmonics.shape[1]
    tv = samples * variables
    halves = cells // LANES
    padded = (halves, tv, lines + 2 * PAD, LANES)
    smem = pl.BlockSpec(memory_space=pltpu.SMEM)
    vmem = pl.BlockSpec(memory_space=pltpu.VMEM)
    hbm = pl.BlockSpec(memory_space=pl.ANY)
    f32 = jnp.float32
    work = SECTIONS * 40 * tv * lines * cells
    moved = 4 * lines * cells * (2 * tv + variables * variables)
    result = pl.pallas_call(
        functools.partial(kernel, rows, n, samples, variables, count),
        out_shape=jax.ShapeDtypeStruct((tv, lines, cells), f32),
        in_specs=[hbm, hbm, smem, smem, smem, vmem, vmem],
        out_specs=hbm,
        scratch_shapes=[
            pltpu.VMEM(padded, f32),
            pltpu.VMEM(padded, f32),
            pltpu.VMEM(padded, f32),
            pltpu.VMEM((halves, variables, variables, lines, LANES), f32),
            pltpu.VMEM((tv, lines, LANES), f32),
            pltpu.VMEM((SECTIONS, variables, variables, SUB, LANES), f32),
            pltpu.VMEM((lines, LANES), f32),
            pltpu.VMEM((lines, LANES), f32),
            pltpu.VMEM((LANES, LANES), f32),
            pltpu.VMEM((SECTIONS, 2, halves, tv, HALO, LANES), f32),
            pltpu.VMEM((SECTIONS, 2, halves, tv, HALO, LANES), f32),
            pltpu.SemaphoreType.DMA((halves,)),
            pltpu.SemaphoreType.DMA((halves,)),
            pltpu.SemaphoreType.DMA((halves,)),
            pltpu.SemaphoreType.DMA((SECTIONS, 2)),
            pltpu.SemaphoreType.DMA((SECTIONS, 2)),
            pltpu.SemaphoreType.DMA,
            pltpu.SemaphoreType.DMA,
        ],
        compiler_params=pltpu.CompilerParams(
            collective_id=0, has_side_effects=True, vmem_limit_bytes=32 * 1024 * 1024),
        cost_estimate=pl.CostEstimate(flops=work, bytes_accessed=moved, transcendentals=0),
    )(
        state.reshape(tv, lines, cells),
        inverse_blocks.reshape(variables, variables, lines, cells),
        flux_jacobian, harmonics, interface_delay, inflow, pairing,
    )
    return result.reshape(state.shape)


def solution(mesh):
    return jax.shard_map(
        functools.partial(body, mesh.shape["row"], mesh.shape["mesh"]),
        mesh=mesh,
        in_specs=(
            P("row", None, None, "mesh", None),
            P("row", None, None, "mesh", None),
            P("row", None, None),
            P(),
            P(),
            P(None, None, "mesh"),
            P("row", "mesh"),
        ),
        out_specs=P("row", None, None, "mesh", None),
        check_vma=False,
    )
```

```python
import functools
import math

import jax
import jax.numpy as jnp
from jax import lax
from jax.experimental import pallas as pl
from jax.experimental.pallas import tpu as pltpu
from jax.sharding import PartitionSpec as P

SECTIONS = 3
nu_second = 0.25
nu_fourth = 0.03
time_scale = 0.05
LANES = 128
SUB = 8
PAD = 8
HALO = 2
MESH = pl.DeviceIdType.MESH


def derivative_coefficients(harm, row, samples, count):
    modes = [harm[row, j] for j in range(count)]
    result = []
    for d in range(1, samples // 2 + 1):
        total = jnp.float32(0.0)
        for n in modes:
            left = lax.rem(n, jnp.int32(samples))
            sine = jnp.float32(0.0)
            for r in range(1, count + 1):
                value = math.sin(2.0 * math.pi * ((r * d) % samples) / samples)
                sine = jnp.where(left == r, jnp.float32(value), sine)
            total = total + n.astype(jnp.float32) * sine
        result.append(total * jnp.float32(-4.0 * math.pi / samples))
    return result


def transfer_matrix(harm, upstream, delay, samples, variables, count):
    used = samples * variables
    high = -(-used // SUB) * SUB
    i = lax.broadcasted_iota(jnp.int32, (high, LANES), 0)
    j = lax.broadcasted_iota(jnp.int32, (high, LANES), 1)
    t = j // variables
    s = i // variables
    same = (i - s * variables == j - t * variables) & (i < used) & (j < used)
    total = jnp.full((high, LANES), 1.0 / samples, jnp.float32)
    for k in range(count):
        n = harm[upstream, k]
        shift = n.astype(jnp.float32) * delay
        steps = n * (t - s + samples)
        steps = steps - samples * (steps // samples)
        turns = steps.astype(jnp.float32) * (1.0 / samples) + shift
        turns = turns - jnp.floor(turns)
        total = total + (2.0 / samples) * jnp.cos((2.0 * math.pi) * turns)
    total = jnp.where(same, total, 0.0)
    return jnp.concatenate([total, jnp.zeros((LANES - high, LANES), jnp.float32)], axis=0)


def kernel(rows, n, samples, variables, count,
           state, inverse, flux_hbm, harm_hbm, delay_hbm, inflow_hbm, pairing_hbm, out,
           q0, qa, qb, iv, ghost, mixing, xout, xin, flow, send, recv,
           flux, harm, delay, inflow, pairing, final,
           load_sem, iv_sem, small_sem, out_sem, send_sem, recv_sem, xsend_sem, xrecv_sem):
    halves, _, _, lines, _ = iv.shape[0], iv.shape[1], iv.shape[2], iv.shape[3], iv.shape[4]
    tv = samples * variables
    tiles = lines // SUB
    row = lax.axis_index("row")
    me = lax.axis_index("mesh")
    has_down = me > 0
    has_up = me < n - 1
    has_before = row > 0
    has_after = row < rows - 1
    down, up, before, after = {"mesh": me - 1}, {"mesh": me + 1}, {"row": row - 1}, {"row": row + 1}
    ways = ((has_down, down), (has_up, up), (has_before, before), (has_after, after))

    barrier = pltpu.get_barrier_semaphore()
    for ok, where in ways:
        @pl.when(ok)
        def _(where=where):
            pl.semaphore_signal(barrier, inc=1, device_id=where, device_id_type=MESH)

    loads = [
        pltpu.make_async_copy(
            state.at[:, :, pl.ds(h * LANES, LANES)],
            q0.at[h, :, pl.ds(PAD, lines), :],
            load_sem.at[h],
        )
        for h in range(halves)
    ]
    iv_loads = [
        pltpu.make_async_copy(
            inverse.at[:, :, :, pl.ds(h * LANES, LANES)], iv.at[h], iv_sem.at[h]
        )
        for h in range(halves)
    ]
    small = [
        pltpu.make_async_copy(source, target, small_sem.at[i])
        for i, (source, target) in enumerate((
            (flux_hbm, flux), (harm_hbm, harm), (delay_hbm, delay),
            (inflow_hbm, inflow), (pairing_hbm, pairing)))
    ]
    for copy in reversed(loads):
        copy.start()
    for copy in small + iv_loads:
        copy.start()

    zeros = jnp.zeros((tv, PAD, LANES), jnp.float32)
    for q in (qa, qb, q0):
        for h in range(halves):
            q[h, :, 0:PAD, :] = zeros
            q[h, :, PAD + lines : 2 * PAD + lines, :] = zeros

    for copy in reversed(loads):
        copy.wait()

    lane = lax.broadcasted_iota(jnp.int32, (lines, LANES), 1)
    packed = jnp.zeros((lines, LANES), jnp.float32)
    for i in range(tv):
        column = pltpu.roll(q0[halves - 1, i, PAD : PAD + lines, :], (i + 1) % LANES, 1)
        packed = jnp.where(lane == i, column, packed)
    xout[...] = packed

    def copies(s):
        first = pltpu.make_async_remote_copy(
            src_ref=send.at[s, 0], dst_ref=recv.at[s, 1], send_sem=send_sem.at[s, 0],
            recv_sem=recv_sem.at[s, 1], device_id=down, device_id_type=MESH)
        last = pltpu.make_async_remote_copy(
            src_ref=send.at[s, 1], dst_ref=recv.at[s, 0], send_sem=send_sem.at[s, 1],
            recv_sem=recv_sem.at[s, 0], device_id=up, device_id_type=MESH)
        return first, last

    def pack_down(s, q):
        for h in range(halves):
            send[s, 0, h] = q[h, :, PAD : PAD + HALO, :]

    def pack_up(s, q):
        for h in range(halves):
            send[s, 1, h] = q[h, :, PAD + lines - HALO : PAD + lines, :]

    def start_down(s):
        pl.when(has_down)(copies(s)[0].start)

    def start_up(s):
        pl.when(has_up)(copies(s)[1].start)

    def finish_down(s, q):
        @pl.when(has_down)
        def _():
            copies(s)[1].wait_recv()
            for h in range(halves):
                q[h, :, PAD - HALO : PAD, :] = recv[s, 0, h]

    def finish_up(s, q):
        @pl.when(has_up)
        def _():
            copies(s)[0].wait_recv()
            for h in range(halves):
                q[h, :, PAD + lines : PAD + lines + HALO, :] = recv[s, 1, h]

    pack_down(0, q0)
    pack_up(0, q0)
    across = pltpu.make_async_remote_copy(
        src_ref=xout, dst_ref=xin, send_sem=xsend_sem, recv_sem=xrecv_sem,
        device_id=after, device_id_type=MESH)

    greeted = sum(ok.astype(jnp.int32) for ok, _ in ways)
    pl.semaphore_wait(barrier, greeted)
    pl.when(has_after)(across.start)
    start_down(0)
    start_up(0)

    for copy in small:
        copy.wait()
    weights = [(s + 1.0) / SECTIONS for s in range(SECTIONS)]
    for s in range(SECTIONS):
        for b in range(variables):
            for a in range(variables):
                mixing[s, b, a] = jnp.full((SUB, LANES), flux[a, 0, b] * jnp.float32(weights[s]), jnp.float32)
    slopes = derivative_coefficients(harm, row, samples, count)
    to_ghost = transfer_matrix(harm, jnp.maximum(row - 1, 0), delay[row], samples, variables, count)
    chosen = (
        jnp.broadcast_to(pairing[...] - me * lines, (lines, lines))
        == lax.broadcasted_iota(jnp.int32, (lines, lines), 0)
    ).astype(jnp.float32)

    @pl.when(row == 0)
    def _():
        flow[...] = jnp.zeros((LANES, LANES), jnp.float32)
        for t in range(samples):
            for v in range(variables):
                flow[t * variables + v : t * variables + v + 1, 0:lines] = inflow[v, t : t + 1]
        xin[...] = jnp.transpose(flow[...])[0:lines, :]

    @pl.when(has_before)
    def _():
        across.wait_recv()

    paired = lax.dot_general(
        chosen, xin[...], (((0,), (0,)), ((), ())),
        precision=lax.Precision.HIGHEST, preferred_element_type=jnp.float32)
    shifted = jnp.dot(
        paired, to_ghost, precision=lax.Precision.HIGHEST, preferred_element_type=jnp.float32)
    for i in range(tv):
        ghost[i] = pltpu.roll(shifted, (LANES - i) % LANES, 1)
    for copy in iv_loads:
        copy.wait()

    at_start = lax.broadcasted_iota(jnp.int32, (variables, SUB, LANES), 2) == 0

    def tile(s, k, src, dst):
        w = weights[s]
        k0 = jnp.float32(w * (2.0 * nu_second + 6.0 * nu_fourth))
        k1 = jnp.float32(w * (-nu_second - 4.0 * nu_fourth))
        k2 = jnp.float32(w * nu_fourth)
        turn = [e * jnp.float32(time_scale * w) for e in slopes]
        line, base = k * SUB, PAD + k * SUB
        if not isinstance(k, int):
            line, base = pl.multiple_of(line, SUB), pl.multiple_of(base, SUB)
        for t in range(samples):
            own = pl.ds(t * variables, variables)
            lower = ghost[own, pl.ds(line, SUB), :]
            for h in range(halves):
                centre = src[h, own, pl.ds(base, SUB), :]
                rolled = pltpu.roll(centre, 1, 2)
                step = centre - jnp.where(at_start, lower, rolled)
                lower = rolled
                total = k0 * centre
                total = total + k1 * (src[h, own, pl.ds(base - 1, SUB), :] + src[h, own, pl.ds(base + 1, SUB), :])
                total = total + k2 * (src[h, own, pl.ds(base - 2, SUB), :] + src[h, own, pl.ds(base + 2, SUB), :])
                for d, slope in enumerate(turn, 1):
                    earlier = pl.ds(((t - d) % samples) * variables, variables)
                    later = pl.ds(((t + d) % samples) * variables, variables)
                    total = total + slope * (
                        src[h, earlier, pl.ds(base, SUB), :] - src[h, later, pl.ds(base, SUB), :])
                for b in range(variables):
                    total = total + mixing[s, b] * step[b : b + 1]
                new = q0[h, own, pl.ds(base, SUB), :]
                for c in range(variables):
                    new = new - iv[h, :, c, pl.ds(line, SUB), :] * total[c : c + 1]
                if dst is None:
                    final[own, pl.ds(line, SUB), h * LANES : (h + 1) * LANES] = new
                else:
                    dst[h, own, pl.ds(base, SUB), :] = new

    stores = [
        pltpu.make_async_copy(final.at[:, part, :], out.at[:, part, :], out_sem.at[i])
        for i, part in enumerate((pl.ds(SUB, lines - 2 * SUB), pl.ds(0, SUB), pl.ds(lines - SUB, SUB)))
    ]

    def section(s, src, dst):
        @pl.loop(1, tiles - 1)
        def _(k):
            tile(s, k, src, dst)

        if dst is None:
            stores[0].start()
        finish_down(s, src)
        tile(s, 0, src, dst)
        if dst is None:
            stores[1].start()
        if s < SECTIONS - 1:
            pack_down(s + 1, dst)
            start_down(s + 1)
        finish_up(s, src)
        tile(s, tiles - 1, src, dst)
        if dst is None:
            stores[2].start()
        if s < SECTIONS - 1:
            pack_up(s + 1, dst)
            start_up(s + 1)

    section(0, q0, qa)
    section(1, qa, qb)
    section(2, qb, None)

    for s in range(SECTIONS):
        first, last = copies(s)
        pl.when(has_down)(first.wait_send)
        pl.when(has_up)(last.wait_send)
    pl.when(has_after)(across.wait_send)
    for copy in stores:
        copy.wait()


def body(rows, n, state, inverse_blocks, flux_jacobian, harmonics, interface_delay, inflow, pairing):
    _, samples, variables, lines, cells = state.shape
    count = harmonics.shape[1]
    tv = samples * variables
    halves = cells // LANES
    padded = (halves, tv, lines + 2 * PAD, LANES)
    hbm = pl.BlockSpec(memory_space=pltpu.HBM)
    f32 = jnp.float32
    work = SECTIONS * 40 * tv * lines * cells
    moved = 4 * lines * cells * (2 * tv + variables * variables)
    result = pl.pallas_call(
        functools.partial(kernel, rows, n, samples, variables, count),
        out_shape=jax.ShapeDtypeStruct((tv, lines, cells), f32),
        in_specs=[hbm] * 7,
        out_specs=hbm,
        scratch_shapes=[
            pltpu.VMEM(padded, f32),
            pltpu.VMEM(padded, f32),
            pltpu.VMEM(padded, f32),
            pltpu.VMEM((halves, variables, variables, lines, LANES), f32),
            pltpu.VMEM((tv, lines, LANES), f32),
            pltpu.VMEM((SECTIONS, variables, variables, SUB, LANES), f32),
            pltpu.VMEM((lines, LANES), f32),
            pltpu.VMEM((lines, LANES), f32),
            pltpu.VMEM((LANES, LANES), f32),
            pltpu.VMEM((SECTIONS, 2, halves, tv, HALO, LANES), f32),
            pltpu.VMEM((SECTIONS, 2, halves, tv, HALO, LANES), f32),
            pltpu.SMEM((variables, 1, variables), f32),
            pltpu.SMEM(harmonics.shape, jnp.int32),
            pltpu.SMEM(interface_delay.shape, f32),
            pltpu.VMEM((variables, samples, lines), f32),
            pltpu.VMEM(pairing.shape, jnp.int32),
            pltpu.VMEM((tv, lines, cells), f32),
            pltpu.SemaphoreType.DMA((halves,)),
            pltpu.SemaphoreType.DMA((halves,)),
            pltpu.SemaphoreType.DMA((5,)),
            pltpu.SemaphoreType.DMA((3,)),
            pltpu.SemaphoreType.DMA((SECTIONS, 2)),
            pltpu.SemaphoreType.DMA((SECTIONS, 2)),
            pltpu.SemaphoreType.DMA,
            pltpu.SemaphoreType.DMA,
        ],
        compiler_params=pltpu.CompilerParams(
            collective_id=0, has_side_effects=True),
        cost_estimate=pl.CostEstimate(flops=work, bytes_accessed=moved, transcendentals=0),
    )(
        state.reshape(tv, lines, cells),
        inverse_blocks.reshape(variables, variables, lines, cells),
        jnp.transpose(flux_jacobian, (1, 0, 2)), harmonics, interface_delay,
        jnp.transpose(inflow, (1, 0, 2)), pairing,
    )
    return result.reshape(state.shape)


def solution(mesh):
    return jax.shard_map(
        functools.partial(body, mesh.shape["row"], mesh.shape["mesh"]),
        mesh=mesh,
        in_specs=(
            P("row", None, None, "mesh", None),
            P("row", None, None, "mesh", None),
            P("row", None, None),
            P(),
            P(),
            P(None, None, "mesh"),
            P("row", "mesh"),
        ),
        out_specs=P("row", None, None, "mesh", None),
        check_vma=False,
    )
```

```python
import functools
import math

import jax
import jax.numpy as jnp
from jax import lax
from jax.experimental import pallas as pl
from jax.experimental.pallas import tpu as pltpu
from jax.sharding import PartitionSpec as P

SECTIONS = 3
nu_second = 0.25
nu_fourth = 0.03
time_scale = 0.05
LANES = 128
SUB = 8
PAD = 8
HALO = 2
MESH = pl.DeviceIdType.MESH


def derivative_coefficients(harm, row, samples, count):
    modes = [harm[row, j] for j in range(count)]
    result = []
    for d in range(1, samples // 2 + 1):
        total = jnp.float32(0.0)
        for n in modes:
            left = lax.rem(n, jnp.int32(samples))
            sine = jnp.float32(0.0)
            for r in range(1, count + 1):
                value = math.sin(2.0 * math.pi * ((r * d) % samples) / samples)
                sine = jnp.where(left == r, jnp.float32(value), sine)
            total = total + n.astype(jnp.float32) * sine
        result.append(total * jnp.float32(-4.0 * math.pi / samples))
    return result


def transfer_matrix(harm, upstream, delay, samples, variables, count):
    used = samples * variables
    high = -(-used // SUB) * SUB
    i = lax.broadcasted_iota(jnp.int32, (high, LANES), 0)
    j = lax.broadcasted_iota(jnp.int32, (high, LANES), 1)
    t = j // variables
    s = i // variables
    same = (i - s * variables == j - t * variables) & (i < used) & (j < used)
    total = jnp.full((high, LANES), 1.0 / samples, jnp.float32)
    for k in range(count):
        n = harm[upstream, k]
        shift = n.astype(jnp.float32) * delay
        steps = n * (t - s + samples)
        steps = steps - samples * (steps // samples)
        turns = steps.astype(jnp.float32) * (1.0 / samples) + shift
        turns = turns - jnp.floor(turns)
        total = total + (2.0 / samples) * jnp.cos((2.0 * math.pi) * turns)
    total = jnp.where(same, total, 0.0)
    return jnp.concatenate([total, jnp.zeros((LANES - high, LANES), jnp.float32)], axis=0)


def kernel(rows, n, samples, variables, count,
           state, inverse, flux_hbm, harm_hbm, delay_hbm, inflow_hbm, pairing_hbm, out,
           q0, qa, qb, iv, ghost, mixing, xout, xin, flow, send, recv,
           flux, harm, delay, inflow, pairing,
           load_sem, iv_sem, small_sem, send_sem, recv_sem, xsend_sem, xrecv_sem):
    halves, _, _, lines, _ = iv.shape
    tv = samples * variables
    tiles = lines // SUB
    row = lax.axis_index("row")
    me = lax.axis_index("mesh")
    has_down = me > 0
    has_up = me < n - 1
    has_before = row > 0
    has_after = row < rows - 1
    down, up, before, after = {"mesh": me - 1}, {"mesh": me + 1}, {"row": row - 1}, {"row": row + 1}
    ways = ((has_down, down), (has_up, up), (has_before, before), (has_after, after))

    barrier = pltpu.get_barrier_semaphore()
    for ok, where in ways:
        @pl.when(ok)
        def _(where=where):
            pl.semaphore_signal(barrier, inc=1, device_id=where, device_id_type=MESH)

    loads = [
        pltpu.make_async_copy(
            state.at[:, :, pl.ds(h * LANES, LANES)],
            q0.at[h, :, pl.ds(PAD, lines), :],
            load_sem.at[h],
        )
        for h in range(halves)
    ]
    iv_loads = [
        pltpu.make_async_copy(
            inverse.at[:, :, :, pl.ds(h * LANES, LANES)], iv.at[h], iv_sem.at[h]
        )
        for h in range(halves)
    ]
    small = [
        pltpu.make_async_copy(source, target, small_sem.at[i])
        for i, (source, target) in enumerate((
            (flux_hbm, flux), (harm_hbm, harm), (delay_hbm, delay),
            (inflow_hbm, inflow), (pairing_hbm, pairing)))
    ]
    for copy in reversed(loads):
        copy.start()
    for copy in small + iv_loads:
        copy.start()

    for copy in reversed(loads):
        copy.wait()

    def copies(s):
        first = pltpu.make_async_remote_copy(
            src_ref=send.at[s, 0], dst_ref=recv.at[s, 1], send_sem=send_sem.at[s, 0],
            recv_sem=recv_sem.at[s, 1], device_id=down, device_id_type=MESH)
        last = pltpu.make_async_remote_copy(
            src_ref=send.at[s, 1], dst_ref=recv.at[s, 0], send_sem=send_sem.at[s, 1],
            recv_sem=recv_sem.at[s, 0], device_id=up, device_id_type=MESH)
        return first, last

    def pack_down(s, q):
        for h in range(halves):
            send[s, 0, h] = q[h, :, PAD : PAD + HALO, :]

    def pack_up(s, q):
        for h in range(halves):
            send[s, 1, h] = q[h, :, PAD + lines - HALO : PAD + lines, :]

    def start_down(s):
        pl.when(has_down)(copies(s)[0].start)

    def start_up(s):
        pl.when(has_up)(copies(s)[1].start)

    def finish_down(s, q):
        @pl.when(has_down)
        def _():
            copies(s)[1].wait_recv()
            for h in range(halves):
                q[h, :, PAD - HALO : PAD, :] = recv[s, 0, h]

    def finish_up(s, q):
        @pl.when(has_up)
        def _():
            copies(s)[0].wait_recv()
            for h in range(halves):
                q[h, :, PAD + lines : PAD + lines + HALO, :] = recv[s, 1, h]

    pack_down(0, q0)
    pack_up(0, q0)
    across = pltpu.make_async_remote_copy(
        src_ref=xout, dst_ref=xin, send_sem=xsend_sem, recv_sem=xrecv_sem,
        device_id=after, device_id_type=MESH)

    greeted = sum(ok.astype(jnp.int32) for ok, _ in ways)
    pl.semaphore_wait(barrier, greeted)
    start_down(0)
    start_up(0)
    lane = lax.broadcasted_iota(jnp.int32, (lines, LANES), 1)
    packed = jnp.zeros((lines, LANES), jnp.float32)
    for i in range(tv):
        column = pltpu.roll(q0[halves - 1, i, PAD : PAD + lines, :], (i + 1) % LANES, 1)
        packed = jnp.where(lane == i, column, packed)
    xout[...] = packed
    pl.when(has_after)(across.start)

    zeros = jnp.zeros((tv, PAD, LANES), jnp.float32)
    for q in (qa, qb, q0):
        for h in range(halves):
            q[h, :, 0:PAD, :] = zeros
            q[h, :, PAD + lines : 2 * PAD + lines, :] = zeros

    for copy in small:
        copy.wait()
    weights = [(s + 1.0) / SECTIONS for s in range(SECTIONS)]
    for s in range(SECTIONS):
        for b in range(variables):
            for a in range(variables):
                mixing[s, b, a] = jnp.full((SUB, LANES), flux[a, 0, b] * jnp.float32(weights[s]), jnp.float32)
    slopes = derivative_coefficients(harm, row, samples, count)
    to_ghost = transfer_matrix(harm, jnp.maximum(row - 1, 0), delay[row], samples, variables, count)
    chosen = (
        jnp.broadcast_to(pairing[...] - me * lines, (lines, lines))
        == lax.broadcasted_iota(jnp.int32, (lines, lines), 0)
    ).astype(jnp.float32)

    @pl.when(row == 0)
    def _():
        flow[...] = jnp.zeros((LANES, LANES), jnp.float32)
        for t in range(samples):
            for v in range(variables):
                flow[t * variables + v : t * variables + v + 1, 0:lines] = inflow[v, t : t + 1]
        xin[...] = jnp.transpose(flow[...])[0:lines, :]

    @pl.when(has_before)
    def _():
        across.wait_recv()

    paired = lax.dot_general(
        chosen, xin[...], (((0,), (0,)), ((), ())),
        precision=lax.Precision.HIGHEST, preferred_element_type=jnp.float32)
    shifted = jnp.dot(
        paired, to_ghost, precision=lax.Precision.HIGHEST, preferred_element_type=jnp.float32)
    for i in range(tv):
        ghost[i] = pltpu.roll(shifted, (LANES - i) % LANES, 1)
    for copy in iv_loads:
        copy.wait()

    at_start = lax.broadcasted_iota(jnp.int32, (variables, SUB, LANES), 2) == 0

    def tile(s, k, src, dst):
        w = weights[s]
        k0 = jnp.float32(w * (2.0 * nu_second + 6.0 * nu_fourth))
        k1 = jnp.float32(w * (-nu_second - 4.0 * nu_fourth))
        k2 = jnp.float32(w * nu_fourth)
        turn = [e * jnp.float32(time_scale * w) for e in slopes]
        line, base = k * SUB, PAD + k * SUB
        if not isinstance(k, int):
            line, base = pl.multiple_of(line, SUB), pl.multiple_of(base, SUB)
        for t in range(samples):
            own = pl.ds(t * variables, variables)
            lower = ghost[own, pl.ds(line, SUB), :]
            for h in range(halves):
                centre = src[h, own, pl.ds(base, SUB), :]
                rolled = pltpu.roll(centre, 1, 2)
                step = centre - jnp.where(at_start, lower, rolled)
                lower = rolled
                total = k0 * centre
                total = total + k1 * (src[h, own, pl.ds(base - 1, SUB), :] + src[h, own, pl.ds(base + 1, SUB), :])
                total = total + k2 * (src[h, own, pl.ds(base - 2, SUB), :] + src[h, own, pl.ds(base + 2, SUB), :])
                for d, slope in enumerate(turn, 1):
                    earlier = pl.ds(((t - d) % samples) * variables, variables)
                    later = pl.ds(((t + d) % samples) * variables, variables)
                    total = total + slope * (
                        src[h, earlier, pl.ds(base, SUB), :] - src[h, later, pl.ds(base, SUB), :])
                for b in range(variables):
                    total = total + mixing[s, b] * step[b : b + 1]
                new = q0[h, own, pl.ds(base, SUB), :]
                for c in range(variables):
                    new = new - iv[h, :, c, pl.ds(line, SUB), :] * total[c : c + 1]
                if dst is None:
                    out[own, pl.ds(line, SUB), h * LANES : (h + 1) * LANES] = new
                else:
                    dst[h, own, pl.ds(base, SUB), :] = new

    def section(s, src, dst):
        @pl.loop(1, tiles - 1)
        def _(k):
            tile(s, k, src, dst)

        finish_down(s, src)
        tile(s, 0, src, dst)
        if s < SECTIONS - 1:
            pack_down(s + 1, dst)
            start_down(s + 1)
        finish_up(s, src)
        tile(s, tiles - 1, src, dst)
        if s < SECTIONS - 1:
            pack_up(s + 1, dst)
            start_up(s + 1)

    section(0, q0, qa)
    section(1, qa, qb)
    section(2, qb, None)

    for s in range(SECTIONS):
        first, last = copies(s)
        pl.when(has_down)(first.wait_send)
        pl.when(has_up)(last.wait_send)
    pl.when(has_after)(across.wait_send)


def body(rows, n, state, inverse_blocks, flux_jacobian, harmonics, interface_delay, inflow, pairing):
    _, samples, variables, lines, cells = state.shape
    count = harmonics.shape[1]
    tv = samples * variables
    halves = cells // LANES
    padded = (halves, tv, lines + 2 * PAD, LANES)
    hbm = pl.BlockSpec(memory_space=pltpu.HBM)
    f32 = jnp.float32
    work = SECTIONS * 40 * tv * lines * cells
    moved = 4 * lines * cells * (2 * tv + variables * variables)
    result = pl.pallas_call(
        functools.partial(kernel, rows, n, samples, variables, count),
        out_shape=pltpu.VMEM((tv, lines, cells), f32),
        in_specs=[hbm] * 7,
        out_specs=pl.BlockSpec(memory_space=pltpu.VMEM),
        scratch_shapes=[
            pltpu.VMEM(padded, f32),
            pltpu.VMEM(padded, f32),
            pltpu.VMEM(padded, f32),
            pltpu.VMEM((halves, variables, variables, lines, LANES), f32),
            pltpu.VMEM((tv, lines, LANES), f32),
            pltpu.VMEM((SECTIONS, variables, variables, SUB, LANES), f32),
            pltpu.VMEM((lines, LANES), f32),
            pltpu.VMEM((lines, LANES), f32),
            pltpu.VMEM((LANES, LANES), f32),
            pltpu.VMEM((SECTIONS, 2, halves, tv, HALO, LANES), f32),
            pltpu.VMEM((SECTIONS, 2, halves, tv, HALO, LANES), f32),
            pltpu.SMEM((variables, 1, variables), f32),
            pltpu.SMEM(harmonics.shape, jnp.int32),
            pltpu.SMEM(interface_delay.shape, f32),
            pltpu.VMEM((variables, samples, lines), f32),
            pltpu.VMEM(pairing.shape, jnp.int32),
            pltpu.SemaphoreType.DMA((halves,)),
            pltpu.SemaphoreType.DMA((halves,)),
            pltpu.SemaphoreType.DMA((5,)),
            pltpu.SemaphoreType.DMA((SECTIONS, 2)),
            pltpu.SemaphoreType.DMA((SECTIONS, 2)),
            pltpu.SemaphoreType.DMA,
            pltpu.SemaphoreType.DMA,
        ],
        compiler_params=pltpu.CompilerParams(
            collective_id=0, has_side_effects=True),
        cost_estimate=pl.CostEstimate(flops=work, bytes_accessed=moved, transcendentals=0),
    )(
        state.reshape(tv, lines, cells),
        inverse_blocks.reshape(variables, variables, lines, cells),
        jnp.transpose(flux_jacobian, (1, 0, 2)), harmonics, interface_delay,
        jnp.transpose(inflow, (1, 0, 2)), pairing,
    )
    return result.reshape(state.shape)


def solution(mesh):
    return jax.shard_map(
        functools.partial(body, mesh.shape["row"], mesh.shape["mesh"]),
        mesh=mesh,
        in_specs=(
            P("row", None, None, "mesh", None),
            P("row", None, None, "mesh", None),
            P("row", None, None),
            P(),
            P(),
            P(None, None, "mesh"),
            P("row", "mesh"),
        ),
        out_specs=P("row", None, None, "mesh", None),
        check_vma=False,
    )
```

```python
import functools
import math

import jax
import jax.numpy as jnp
from jax import lax
from jax.experimental import pallas as pl
from jax.experimental.pallas import tpu as pltpu
from jax.sharding import PartitionSpec as P

SECTIONS = 3
nu_second = 0.25
nu_fourth = 0.03
time_scale = 0.05
LANES = 128
SUB = 8
PAD = 8
HALO = 2
MESH = pl.DeviceIdType.MESH


def derivative_coefficients(harm, row, samples, count):
    modes = [harm[row, j] for j in range(count)]
    result = []
    for d in range(1, samples // 2 + 1):
        total = jnp.float32(0.0)
        for n in modes:
            left = lax.rem(n, jnp.int32(samples))
            sine = jnp.float32(0.0)
            for r in range(1, count + 1):
                value = math.sin(2.0 * math.pi * ((r * d) % samples) / samples)
                sine = jnp.where(left == r, jnp.float32(value), sine)
            total = total + n.astype(jnp.float32) * sine
        result.append(total * jnp.float32(-4.0 * math.pi / samples))
    return result


def transfer_matrix(harm, upstream, delay, samples, variables, count):
    used = samples * variables
    high = -(-used // SUB) * SUB
    i = lax.broadcasted_iota(jnp.int32, (high, LANES), 0)
    j = lax.broadcasted_iota(jnp.int32, (high, LANES), 1)
    t = j // variables
    s = i // variables
    same = (i - s * variables == j - t * variables) & (i < used) & (j < used)
    total = jnp.full((high, LANES), 1.0 / samples, jnp.float32)
    for k in range(count):
        n = harm[upstream, k]
        shift = n.astype(jnp.float32) * delay
        steps = n * (t - s + samples)
        steps = steps - samples * (steps // samples)
        turns = steps.astype(jnp.float32) * (1.0 / samples) + shift
        turns = turns - jnp.floor(turns)
        total = total + (2.0 / samples) * jnp.cos((2.0 * math.pi) * turns)
    total = jnp.where(same, total, 0.0)
    return jnp.concatenate([total, jnp.zeros((LANES - high, LANES), jnp.float32)], axis=0)


def kernel(rows, n, samples, variables, count,
           state, inverse, flux_hbm, harm_hbm, delay_hbm, inflow_hbm, pairing_hbm, out,
           q0, qa, qb, iv, ghost, mixing, xout, xin, flow, send, recv,
           flux, harm, delay, inflow, pairing,
           load_sem, iv_sem, small_sem, send_sem, recv_sem, xsend_sem, xrecv_sem):
    halves, _, _, lines, _ = iv.shape
    tv = samples * variables
    tiles = lines // SUB
    row = lax.axis_index("row")
    me = lax.axis_index("mesh")
    has_down = me > 0
    has_up = me < n - 1
    has_before = row > 0
    has_after = row < rows - 1
    down, up, before, after = {"mesh": me - 1}, {"mesh": me + 1}, {"row": row - 1}, {"row": row + 1}
    ways = ((has_down, down), (has_up, up), (has_before, before), (has_after, after))

    barrier = pltpu.get_barrier_semaphore()
    for ok, where in ways:
        @pl.when(ok)
        def _(where=where):
            pl.semaphore_signal(barrier, inc=1, device_id=where, device_id_type=MESH)

    loads = [
        pltpu.make_async_copy(
            state.at[:, :, pl.ds(h * LANES, LANES)],
            q0.at[h, :, pl.ds(PAD, lines), :],
            load_sem.at[h],
        )
        for h in range(halves)
    ]
    iv_loads = [
        pltpu.make_async_copy(
            inverse.at[:, :, :, pl.ds(h * LANES, LANES)], iv.at[h], iv_sem.at[h]
        )
        for h in range(halves)
    ]
    small = [
        pltpu.make_async_copy(source, target, small_sem.at[i])
        for i, (source, target) in enumerate((
            (flux_hbm, flux), (harm_hbm, harm), (delay_hbm, delay),
            (inflow_hbm, inflow), (pairing_hbm, pairing)))
    ]
    for copy in reversed(loads):
        copy.start()
    for copy in small + iv_loads:
        copy.start()

    for copy in reversed(loads):
        copy.wait()

    def copies(s):
        first = pltpu.make_async_remote_copy(
            src_ref=send.at[s, 0], dst_ref=recv.at[s, 1], send_sem=send_sem.at[s, 0],
            recv_sem=recv_sem.at[s, 1], device_id=down, device_id_type=MESH)
        last = pltpu.make_async_remote_copy(
            src_ref=send.at[s, 1], dst_ref=recv.at[s, 0], send_sem=send_sem.at[s, 1],
            recv_sem=recv_sem.at[s, 0], device_id=up, device_id_type=MESH)
        return first, last

    def pack_down(s, q):
        for h in range(halves):
            send[s, 0, h] = q[h, :, PAD : PAD + HALO, :]

    def pack_up(s, q):
        for h in range(halves):
            send[s, 1, h] = q[h, :, PAD + lines - HALO : PAD + lines, :]

    def start_down(s):
        pl.when(has_down)(copies(s)[0].start)

    def start_up(s):
        pl.when(has_up)(copies(s)[1].start)

    def finish_down(s, q):
        @pl.when(has_down)
        def _():
            copies(s)[1].wait_recv()
            for h in range(halves):
                q[h, :, PAD - HALO : PAD, :] = recv[s, 0, h]

    def finish_up(s, q):
        @pl.when(has_up)
        def _():
            copies(s)[0].wait_recv()
            for h in range(halves):
                q[h, :, PAD + lines : PAD + lines + HALO, :] = recv[s, 1, h]

    pack_down(0, q0)
    pack_up(0, q0)
    across = pltpu.make_async_remote_copy(
        src_ref=xout, dst_ref=xin, send_sem=xsend_sem, recv_sem=xrecv_sem,
        device_id=after, device_id_type=MESH)

    greeted = sum(ok.astype(jnp.int32) for ok, _ in ways)
    pl.semaphore_wait(barrier, greeted)
    start_down(0)
    start_up(0)
    lane = lax.broadcasted_iota(jnp.int32, (lines, LANES), 1)
    packed = jnp.zeros((lines, LANES), jnp.float32)
    for i in range(tv):
        column = pltpu.roll(q0[halves - 1, i, PAD : PAD + lines, :], (i + 1) % LANES, 1)
        packed = jnp.where(lane == i, column, packed)
    xout[...] = packed
    pl.when(has_after)(across.start)

    zeros = jnp.zeros((tv, PAD, LANES), jnp.float32)
    for q in (qa, qb, q0):
        for h in range(halves):
            q[h, :, 0:PAD, :] = zeros
            q[h, :, PAD + lines : 2 * PAD + lines, :] = zeros

    for copy in small:
        copy.wait()
    weights = [(s + 1.0) / SECTIONS for s in range(SECTIONS)]
    for s in range(SECTIONS):
        for b in range(variables):
            for a in range(variables):
                mixing[s, b, a] = jnp.full((SUB, LANES), flux[a, 0, b] * jnp.float32(weights[s]), jnp.float32)
    slopes = derivative_coefficients(harm, row, samples, count)
    to_ghost = transfer_matrix(harm, jnp.maximum(row - 1, 0), delay[row], samples, variables, count)
    chosen = (
        jnp.broadcast_to(pairing[...] - me * lines, (lines, lines))
        == lax.broadcasted_iota(jnp.int32, (lines, lines), 0)
    ).astype(jnp.float32)

    @pl.when(row == 0)
    def _():
        flow[...] = jnp.zeros((LANES, LANES), jnp.float32)
        for t in range(samples):
            for v in range(variables):
                flow[t * variables + v : t * variables + v + 1, 0:lines] = inflow[v, t : t + 1]
        xin[...] = jnp.transpose(flow[...])[0:lines, :]

    @pl.when(has_before)
    def _():
        across.wait_recv()

    paired = lax.dot_general(
        chosen, xin[...], (((0,), (0,)), ((), ())),
        precision=lax.Precision.HIGHEST, preferred_element_type=jnp.float32)
    shifted = jnp.dot(
        paired, to_ghost, precision=lax.Precision.HIGHEST, preferred_element_type=jnp.float32)
    for i in range(tv):
        ghost[i] = pltpu.roll(shifted, (LANES - i) % LANES, 1)
    for copy in iv_loads:
        copy.wait()

    at_start = lax.broadcasted_iota(jnp.int32, (variables, SUB, LANES), 2) == 0

    def tile(s, k, src, dst):
        w = weights[s]
        k0 = jnp.float32(w * (2.0 * nu_second + 6.0 * nu_fourth))
        k1 = jnp.float32(w * (-nu_second - 4.0 * nu_fourth))
        k2 = jnp.float32(w * nu_fourth)
        turn = [e * jnp.float32(time_scale * w) for e in slopes]
        line, base = k * SUB, PAD + k * SUB
        if not isinstance(k, int):
            line, base = pl.multiple_of(line, SUB), pl.multiple_of(base, SUB)
        for t in range(samples):
            own = pl.ds(t * variables, variables)
            lower = ghost[own, pl.ds(line, SUB), :]
            for h in range(halves):
                centre = src[h, own, pl.ds(base, SUB), :]
                rolled = pltpu.roll(centre, 1, 2)
                step = centre - jnp.where(at_start, lower, rolled)
                lower = rolled
                total = k0 * centre
                total = total + k1 * (src[h, own, pl.ds(base - 1, SUB), :] + src[h, own, pl.ds(base + 1, SUB), :])
                total = total + k2 * (src[h, own, pl.ds(base - 2, SUB), :] + src[h, own, pl.ds(base + 2, SUB), :])
                for d, slope in enumerate(turn, 1):
                    earlier = pl.ds(((t - d) % samples) * variables, variables)
                    later = pl.ds(((t + d) % samples) * variables, variables)
                    total = total + slope * (
                        src[h, earlier, pl.ds(base, SUB), :] - src[h, later, pl.ds(base, SUB), :])
                for b in range(variables):
                    total = total + mixing[s, b] * step[b : b + 1]
                new = q0[h, own, pl.ds(base, SUB), :]
                for c in range(variables):
                    new = new - iv[h, :, c, pl.ds(line, SUB), :] * total[c : c + 1]
                if dst is None:
                    out[own, pl.ds(line, SUB), h * LANES : (h + 1) * LANES] = new
                else:
                    dst[h, own, pl.ds(base, SUB), :] = new

    def section(s, src, dst):
        @pl.loop(1, tiles - 1)
        def _(k):
            tile(s, k, src, dst)

        @pl.loop(0, 2)
        def _(i):
            side = lax.rem(me + 1 + i, 2)
            pl.when(side == 0)(lambda: finish_down(s, src))
            pl.when(side == 1)(lambda: finish_up(s, src))
            tile(s, side * (tiles - 1), src, dst)
            if s < SECTIONS - 1:
                @pl.when(side == 0)
                def _():
                    pack_down(s + 1, dst)
                    start_down(s + 1)

                @pl.when(side == 1)
                def _():
                    pack_up(s + 1, dst)
                    start_up(s + 1)

    section(0, q0, qa)
    section(1, qa, qb)
    section(2, qb, None)

    for s in range(SECTIONS):
        first, last = copies(s)
        pl.when(has_down)(first.wait_send)
        pl.when(has_up)(last.wait_send)
    pl.when(has_after)(across.wait_send)


def body(rows, n, state, inverse_blocks, flux_jacobian, harmonics, interface_delay, inflow, pairing):
    _, samples, variables, lines, cells = state.shape
    count = harmonics.shape[1]
    tv = samples * variables
    halves = cells // LANES
    padded = (halves, tv, lines + 2 * PAD, LANES)
    hbm = pl.BlockSpec(memory_space=pltpu.HBM)
    f32 = jnp.float32
    work = SECTIONS * 40 * tv * lines * cells
    moved = 4 * lines * cells * (2 * tv + variables * variables)
    result = pl.pallas_call(
        functools.partial(kernel, rows, n, samples, variables, count),
        out_shape=pltpu.VMEM((tv, lines, cells), f32),
        in_specs=[hbm] * 7,
        out_specs=pl.BlockSpec(memory_space=pltpu.VMEM),
        scratch_shapes=[
            pltpu.VMEM(padded, f32),
            pltpu.VMEM(padded, f32),
            pltpu.VMEM(padded, f32),
            pltpu.VMEM((halves, variables, variables, lines, LANES), f32),
            pltpu.VMEM((tv, lines, LANES), f32),
            pltpu.VMEM((SECTIONS, variables, variables, SUB, LANES), f32),
            pltpu.VMEM((lines, LANES), f32),
            pltpu.VMEM((lines, LANES), f32),
            pltpu.VMEM((LANES, LANES), f32),
            pltpu.VMEM((SECTIONS, 2, halves, tv, HALO, LANES), f32),
            pltpu.VMEM((SECTIONS, 2, halves, tv, HALO, LANES), f32),
            pltpu.SMEM((variables, 1, variables), f32),
            pltpu.SMEM(harmonics.shape, jnp.int32),
            pltpu.SMEM(interface_delay.shape, f32),
            pltpu.VMEM((variables, samples, lines), f32),
            pltpu.VMEM(pairing.shape, jnp.int32),
            pltpu.SemaphoreType.DMA((halves,)),
            pltpu.SemaphoreType.DMA((halves,)),
            pltpu.SemaphoreType.DMA((5,)),
            pltpu.SemaphoreType.DMA((SECTIONS, 2)),
            pltpu.SemaphoreType.DMA((SECTIONS, 2)),
            pltpu.SemaphoreType.DMA,
            pltpu.SemaphoreType.DMA,
        ],
        compiler_params=pltpu.CompilerParams(
            collective_id=0, has_side_effects=True),
        cost_estimate=pl.CostEstimate(flops=work, bytes_accessed=moved, transcendentals=0),
    )(
        state.reshape(tv, lines, cells),
        inverse_blocks.reshape(variables, variables, lines, cells),
        jnp.transpose(flux_jacobian, (1, 0, 2)), harmonics, interface_delay,
        jnp.transpose(inflow, (1, 0, 2)), pairing,
    )
    return result.reshape(state.shape)


def solution(mesh):
    return jax.shard_map(
        functools.partial(body, mesh.shape["row"], mesh.shape["mesh"]),
        mesh=mesh,
        in_specs=(
            P("row", None, None, "mesh", None),
            P("row", None, None, "mesh", None),
            P("row", None, None),
            P(),
            P(),
            P(None, None, "mesh"),
            P("row", "mesh"),
        ),
        out_specs=P("row", None, None, "mesh", None),
        check_vma=False,
    )
```
